256 devices in a mesh: prow: 8 (over x, core), pcol: 32 (over y, z).
Axes of the slice: x: 4, y: 4, z: 8, core: 2. Of those that a mesh axis runs over, the one named last changes fastest.
Arguments:
- factor_blocks: float32 [6, 4, 8, 32, 256, 256], P(None, None, 'prow', 'pcol'), may hold values from -0.03125 to 0.03125
- block_pattern: int32 [6, 4, 8, 32], P(None, None, 'prow', 'pcol'), may hold values 0 or 1
- right_side: float32 [4, 32, 512, 256], P(None, 'pcol'), may hold values from -6 to 6
- diag_inverse: float32 [4, 32, 256, 256], P(None, 'pcol'), may hold values from -1 to 1.5, as said below
Outputs:
- forward_solution: float32 [4, 32, 512, 256], P(None, 'pcol')
- solution: float32 [4, 32, 512, 256], P(None, 'pcol', 'prow')
The draws below stay inside these ranges and needn't reach their ends.
Inputs may be any that keep to these rules, and one draw needn't show every extreme that they name: Each block of diag_inverse is lower triangular with diagonal entries from 0.5 to 1.5.
All inputs are finite; a program needn't handle non-finite values. No bound on the sum of `block_pattern` on one device may be relied on, other than what follows from the above.
Results may differ from the reference program's by a relative error of at most 0.0001.
Values sent between devices are 32-bit elements; how exact they have to be, the bound alone decides.
No kernel may reach another device: no remote copies, remote signals or barrier semaphores. Data moves between devices by JAX's collectives and lax.ppermute only.
A program may use at most 64 MiB of HBM per device.

```python
import jax
import jax.numpy as jnp
from jax import lax

B = 256
NRHS = 512
LV = 4
SPL = 32
RPL = 4
NPAIR = 6
N_PROW = 8


def draw_diag_inverse(key, part):
    first_key, second_key = jax.random.split(jax.random.fold_in(key, 11))
    full_shape = (LV, SPL, B, B)
    entries = jnp.clip(jax.random.normal(first_key, full_shape, jnp.float32), -2.5, 2.5)
    lower_part = jnp.tril(entries * (0.05 * 256.0 / B), -1)
    diagonal = jax.random.uniform(second_key, (LV, SPL, B), jnp.float32, 0.5, 1.5)
    return lower_part + diagonal[..., None] * jnp.eye(B, dtype=jnp.float32)


def touch_ends(values, stream_key, least, high):
    shape = values.shape
    place = [jax.random.randint(jax.random.fold_in(stream_key, axis), (), 0, shape[axis]) for axis in range(len(shape))]
    values = values.at[tuple(place)].set(least)
    longest = shape.index(max(shape))
    place[longest] = (place[longest] + 1) % shape[longest]
    return values.at[tuple(place)].set(high)


def levels(own_key, extent, shards, low, high):
    level = 1.0
    for axis_at, blocks in shards:
        heights = jax.random.uniform(jax.random.fold_in(jax.random.fold_in(own_key, 6), axis_at), (blocks,), jnp.float32, low / len(shards), high / len(shards))
        level = level * jnp.repeat(jnp.exp(heights), extent[axis_at] // blocks).reshape((-1,) + (1,) * (len(extent) - 1 - axis_at))
    return level


def normal_values(rng, extent, width, reach, pieces=(), kind=jnp.bfloat16):
    drawn = jax.random.normal(rng, extent, jnp.float32) * width
    if len(pieces) > 0:
        drawn = levels(rng, extent, pieces, -0.22, 0.18) * drawn
    return jnp.clip(drawn, min=-reach, max=reach).astype(kind)


def setup_inputs(seed: int = 0) -> dict:
    arg_keys = jax.random.split(jax.random.key(seed), 5)
    return {
        "factor_blocks": normal_values(arg_keys[0], (NPAIR, RPL, N_PROW, SPL, B, B), (B * SPL * LV) ** -0.5, 0.03125, ((2, 8), (3, 32)), jnp.float32),
        "block_pattern": touch_ends((jax.random.randint(arg_keys[1], (NPAIR, RPL, N_PROW, SPL), 0, 3) < 2).astype(jnp.int32), jax.random.fold_in(arg_keys[1], 1), 0, 1),
        "right_side": normal_values(arg_keys[2], (LV, SPL, NRHS, B), 1.0, 6.0, ((1, 32),), jnp.float32),
        "diag_inverse": draw_diag_inverse(jax.random.fold_in(arg_keys[4], 71), 0),
    }


highest = lax.Precision.HIGHEST


def pair_number(later_level, earlier):
    return later_level * (later_level - 1) // 2 + earlier


def masked_pair(factor_blocks, pattern_float, number):
    blocks = factor_blocks[number].reshape(SPL, SPL, B, B)
    weights = pattern_float[number].reshape(SPL, SPL)
    return blocks * weights[:, :, None, None]


def reference(factor_blocks, block_pattern, right_side, diag_inverse):
    pattern_float = block_pattern.astype(jnp.float32)
    forward = []
    for current in range(LV):
        update = jnp.zeros((SPL, NRHS, B), jnp.float32)
        for earlier in range(current):
            masked = masked_pair(factor_blocks, pattern_float, pair_number(current, earlier))
            update = update + jnp.einsum("pkij,knj->pni", masked, forward[earlier], precision=highest)
        solved = jnp.einsum("pnj,pij->pni", right_side[current] - update, diag_inverse[current], precision=highest)
        forward.append(solved)
    backward = [None] * LV
    for current in range(LV - 1, -1, -1):
        update = jnp.zeros((SPL, NRHS, B), jnp.float32)
        for later_level in range(current + 1, LV):
            masked = masked_pair(factor_blocks, pattern_float, pair_number(later_level, current))
            update = update + jnp.einsum("pkij,pni->knj", masked, backward[later_level], precision=highest)
        backward[current] = jnp.einsum("kni,kij->knj", forward[current] - update, diag_inverse[current], precision=highest)
    return jnp.stack(forward), jnp.stack(backward)
```

```python
import jax
import jax.numpy as jnp
from jax import lax
from jax.sharding import PartitionSpec as P

B = 256
NRHS = 512
LV = 4
ROWS = 8
YS = 4
ZS = 8
SHARE = NRHS // ROWS
PREC = lax.Precision.HIGH

Z_GROUPS = [[y * ZS + z for z in range(ZS)] for y in range(YS)]


def first_pair(later_level):
    return later_level * (later_level - 1) // 2


def pair_number(later_level, earlier):
    return first_pair(later_level) + earlier


def y_shift(value, k):
    pairs = [(y * ZS + z, (y + k) % YS * ZS + z) for y in range(YS) for z in range(ZS)]
    return lax.ppermute(value, "pcol", pairs)


def transpose_devices(value):
    columns = YS * ZS
    pairs = [
        (r * columns + y * ZS + z, z * columns + y * ZS + r)
        for r in range(ROWS)
        for y in range(YS)
        for z in range(ZS)
    ]
    return lax.ppermute(value, ("prow", "pcol"), pairs)


def z_exchange(value):
    return lax.all_to_all(value, "pcol", 0, 0, tiled=True, axis_index_groups=Z_GROUPS)


def row_exchange(value):
    return lax.all_to_all(value, "prow", 0, 0, tiled=True)


def dot(left, right, left_axis, right_axis):
    return lax.dot_general(
        left,
        right,
        (((left_axis,), (right_axis,)), ((), ())),
        precision=PREC,
        preferred_element_type=jnp.float32,
    )


def local(factor_blocks, block_pattern, right_side, diag_inverse):
    own_row = lax.axis_index("prow")
    own_y = lax.axis_index("pcol") // ZS
    pattern = block_pattern[:, :, 0, 0].astype(jnp.float32)
    masked = factor_blocks[:, :, 0, 0] * pattern[:, :, None, None]
    blocks = lax.dynamic_slice_in_dim(jnp.concatenate([masked, masked[:, :-1]], axis=1), own_y, YS, 1)
    own_right = right_side[:, 0]
    own_inverse = diag_inverse[:, 0]
    right_share = lax.dynamic_slice_in_dim(own_right, own_row * SHARE, SHARE, 1)

    forward = [dot(own_right[0], own_inverse[0], 1, 1)]
    forward_share = [lax.dynamic_slice_in_dim(forward[0], own_row * SHARE, SHARE, 0)]
    for current in range(1, LV):
        parts = []
        for k in range(YS):
            part = None
            for earlier in range(current):
                term = dot(forward[earlier], blocks[pair_number(current, earlier), k], 1, 1)
                part = term if part is None else part + term
            parts.append(part)
        summed = parts[0] + y_shift(parts[2], 2) + y_shift(parts[1], 1) + y_shift(parts[3], 3)
        arrived = z_exchange(summed.reshape(ZS, SHARE, B)).sum(0)
        arrived = transpose_devices(arrived)
        share = dot(right_share[current] - arrived, own_inverse[current], 1, 1)
        forward_share.append(share)
        forward.append(lax.all_gather(share, "prow", axis=0, tiled=True))

    solution = [None] * LV
    rows_of = [None] * LV
    for current in range(LV - 1, -1, -1):
        update = forward_share[current]
        if current < LV - 1:
            partial_sum = None
            for later_level in range(current + 1, LV):
                number = pair_number(later_level, current)
                for k in range(YS):
                    term = dot(rows_of[later_level][k], blocks[number, k], 1, 0)
                    partial_sum = term if partial_sum is None else partial_sum + term
            update = update - row_exchange(partial_sum.reshape(ROWS, SHARE, B)).sum(0)
        solved = dot(update, own_inverse[current], 1, 0)
        solution[current] = solved
        if current > 0:
            moved = transpose_devices(solved)
            copies = jnp.broadcast_to(moved[None], (ZS, SHARE, B))
            whole = z_exchange(copies).reshape(NRHS, B)
            rows_of[current] = [whole, y_shift(whole, 3), y_shift(whole, 2), y_shift(whole, 1)]
    return (jnp.stack(forward)[:, None], jnp.stack(solution)[:, None])


def solution(mesh):
    in_specs = (
        P(None, None, "prow", "pcol", None, None),
        P(None, None, "prow", "pcol"),
        P(None, "pcol", None, None),
        P(None, "pcol", None, None),
    )
    out_specs = (P(None, "pcol", None, None), P(None, "pcol", "prow", None))
    return jax.shard_map(local, mesh=mesh, in_specs=in_specs, out_specs=out_specs, check_vma=False)
```

```python
import jax
import jax.numpy as jnp
from jax import lax
from jax.sharding import PartitionSpec as P

B = 256
NRHS = 512
LV = 4
ROWS = 8
SHARE = NRHS // ROWS
CHAINS = 1
PART = SHARE // CHAINS
HIGH = lax.Precision.HIGH
HIGHEST = lax.Precision.HIGHEST


def pair_number(later_level, earlier):
    return later_level * (later_level - 1) // 2 + earlier


def send(value, target):
    pairs = []
    for device in range(256):
        row, column = divmod(device, 32)
        there = target(row // 2, row % 2, column // 8, column // 2 % 4, column % 2)
        pairs.append((device, (there[0] * 2 + there[1]) * 32 + there[2] * 8 + there[3] * 2 + there[4]))
    return lax.ppermute(value, ("prow", "pcol"), pairs)


def to_y(value, k):
    return send(value, lambda x, c, y, h, l: (x, c, y ^ k, h, l))


def to_x(value, k):
    return send(value, lambda x, c, y, h, l: (x ^ k, c, y, h, l))


def to_core(value):
    return send(value, lambda x, c, y, h, l: (x, c ^ 1, y, h, l))


def dot(left, right, left_axis, right_axis, precision=HIGH):
    return lax.dot_general(
        left,
        right,
        (((left_axis,), (right_axis,)), ((), ())),
        precision=precision,
        preferred_element_type=jnp.float32,
    )


def pick(value, index, axis):
    return lax.dynamic_index_in_dim(value, index, axis, keepdims=False)


def ordered(items, own):
    low, high = own % 2 == 1, own // 2 == 1
    pairs = [jnp.where(low, items[k ^ 1], items[k]) for k in range(4)]
    return jnp.stack([jnp.where(high, pairs[s ^ 2], pairs[s]) for s in range(4)])


def local(factor_blocks, block_pattern, right_side, diag_inverse):
    row = lax.axis_index("prow")
    column = lax.axis_index("pcol")
    x, core = row // 2, row % 2
    y, zh, zl = column // 8, column // 2 % 4, column % 2
    pattern = block_pattern[:, :, 0, 0].astype(jnp.float32)
    blocks = []
    for number in range(6):
        picked = [pick(factor_blocks[number, :, 0, 0], y ^ k, 0) * pick(pattern[number], y ^ k, 0) for k in range(4)]
        blocks.append(lax.optimization_barrier(picked))
    right = right_side[:, 0].reshape(LV, 4, 2, CHAINS, PART, B)
    inverse = diag_inverse[:, 0]
    right_share = pick(pick(right, x, 1), core, 1)

    def update_to_share(parts):
        moved = [to_y(parts(k), k) for k in (2, 1, 3)]
        total = parts(0)
        for value in moved:
            total = total + value
        arrived = None
        for k in range(2):
            value = send(pick(total, zl ^ k, 1), lambda x, c, y, h, l: (x, l ^ k, y, h, c))
            arrived = value if arrived is None else arrived + value
        total, arrived = arrived, None
        for k in range(4):
            value = send(pick(total, zh ^ k, 0), lambda x, c, y, h, l: (h ^ k, c, y, x, l))
            arrived = value if arrived is None else arrived + value
        return arrived

    def share_to_rows(share):
        items = [send(share, lambda x, c, y, h, l: (h, c, y, x ^ k, l)) for k in range(4)]
        whole = ordered(items, zh)
        halves = [send(whole, lambda x, c, y, h, l: (x, l, y, h, c ^ k)) for k in range(2)]
        whole = jnp.stack([jnp.where(zl == 0, halves[0], halves[1]), jnp.where(zl == 0, halves[1], halves[0])], 1)
        whole = whole.reshape(8 * PART, B)
        moved = {k: to_y(whole, k) for k in (2, 1, 3)}
        return [whole, moved[1], moved[2], moved[3]]

    def gather_rows(share):
        whole = ordered([share] + [to_x(share, k) for k in (1, 2, 3)], x)
        other = to_core(whole)
        whole = jnp.stack([jnp.where(core == 0, whole, other), jnp.where(core == 0, other, whole)], 1)
        return whole.reshape(8 * PART, B)

    def sum_rows(partial_sum):
        view = partial_sum.reshape(4, 2, PART, B)
        total = pick(view, core, 1) + to_core(pick(view, 1 - core, 1))
        moved = [to_x(pick(total, x ^ k, 0), k) for k in (2, 1, 3)]
        arrived = pick(total, x, 0)
        for value in moved:
            arrived = arrived + value
        return arrived

    first = dot(right_side[0, 0], inverse[0], 1, 1, HIGHEST).reshape(8, CHAINS, PART, B)
    forward = [[first[:, chain].reshape(8 * PART, B)] for chain in range(CHAINS)]
    shares = [[pick(first[:, chain], row, 0)] for chain in range(CHAINS)]
    for current in range(1, LV):
        for chain in range(CHAINS):

            def parts(k):
                total = None
                for earlier in range(current):
                    term = dot(forward[chain][earlier], blocks[pair_number(current, earlier)][k], 1, 1)
                    total = term if total is None else total + term
                return total.reshape(4, 2, PART, B)

            arrived = update_to_share(parts)
            share = dot(right_share[current, chain] - arrived, inverse[current], 1, 1, HIGHEST)
            shares[chain].append(share)
            forward[chain].append(gather_rows(share))

    solution = [[None] * LV for _ in range(CHAINS)]
    rows_of = [[None] * LV for _ in range(CHAINS)]
    for current in range(LV - 1, -1, -1):
        for chain in range(CHAINS):
            update = shares[chain][current]
            if current < LV - 1:
                partial_sum = None
                for later_level in range(LV - 1, current, -1):
                    for k in range(4):
                        term = dot(rows_of[chain][later_level][k], blocks[pair_number(later_level, current)][k], 1, 0)
                        partial_sum = term if partial_sum is None else partial_sum + term
                update = update - sum_rows(partial_sum)
            solved = dot(update, inverse[current], 1, 0, HIGHEST)
            solution[chain][current] = solved
            if current > 0:
                rows_of[chain][current] = share_to_rows(solved)

    forward_out = [jnp.stack([forward[c][l].reshape(8, PART, B) for c in range(CHAINS)], 1) for l in range(LV)]
    forward_out = jnp.stack(forward_out).reshape(LV, 1, NRHS, B)
    solution_out = jnp.stack([jnp.concatenate([solution[c][l] for c in range(CHAINS)]) for l in range(LV)])
    return forward_out, solution_out[:, None]


def solution(mesh):
    in_specs = (
        P(None, None, "prow", "pcol", None, None),
        P(None, None, "prow", "pcol"),
        P(None, "pcol", None, None),
        P(None, "pcol", None, None),
    )
    out_specs = (P(None, "pcol", None, None), P(None, "pcol", "prow", None))
    return jax.shard_map(local, mesh=mesh, in_specs=in_specs, out_specs=out_specs, check_vma=False)
```

```python
import jax
import jax.numpy as jnp
from jax import lax
from jax.sharding import PartitionSpec as P

B = 256
NRHS = 512
LV = 4
SHARE = 64
HALF = 256
HIGH = lax.Precision.HIGH
HIGHEST = lax.Precision.HIGHEST


def pair_number(later_level, earlier):
    return later_level * (later_level - 1) // 2 + earlier


def send(value, target):
    pairs = []
    for device in range(256):
        row, column = divmod(device, 32)
        there = target(row // 2, row % 2, column // 8, column // 2 % 4, column % 2)
        pairs.append((device, (there[0] * 2 + there[1]) * 32 + there[2] * 8 + there[3] * 2 + there[4]))
    return lax.ppermute(value, ("prow", "pcol"), pairs)


def to_y(value, k):
    return send(value, lambda x, c, y, h, l: (x, c, y ^ k, h, l))


def to_x(value, k):
    return send(value, lambda x, c, y, h, l: (x ^ k, c, y, h, l))


def to_core(value):
    return send(value, lambda x, c, y, h, l: (x, c ^ 1, y, h, l))


def to_pair(value):
    return send(value, lambda x, c, y, h, l: (x, c, y, h, l ^ 1))


def swap(value):
    return send(value, lambda x, c, y, h, l: (x, l, y, h, c))


def dot(left, right, left_axis, right_axis, precision=HIGH):
    return lax.dot_general(
        left,
        right,
        (((left_axis,), (right_axis,)), ((), ())),
        precision=precision,
        preferred_element_type=jnp.float32,
    )


def pick(value, index, axis):
    return lax.dynamic_index_in_dim(value, index, axis, keepdims=False)


def ordered(items, own):
    low, high = own % 2 == 1, own // 2 == 1
    pairs = [jnp.where(low, items[k ^ 1], items[k]) for k in range(4)]
    return jnp.concatenate([jnp.where(high, pairs[s ^ 2], pairs[s]) for s in range(4)])


def local(factor_blocks, block_pattern, right_side, diag_inverse):
    row = lax.axis_index("prow")
    column = lax.axis_index("pcol")
    x, core = row // 2, row % 2
    y, zh, zl = column // 8, column // 2 % 4, column % 2
    pattern = block_pattern[:, :, 0, 0].astype(jnp.float32)

    def by_pair(own, other, axis):
        return jnp.concatenate([jnp.where(zl == 0, own, other), jnp.where(zl == 0, other, own)], axis)

    blocks = []
    for number in range(6):
        own = factor_blocks[number, :, 0, 0] * pattern[number][:, None, None]
        blocks.append(by_pair(own, to_pair(own), 2))

    right = right_side[:, 0].reshape(LV, 8, SHARE, B)
    moved = swap(pick(right[1:], row, 1).reshape(-1, B))
    right_share = [None] + [moved[i * SHARE : (i + 1) * SHARE] for i in range(3)]
    inverse = swap(diag_inverse[:, 0])

    def update_to_share(parts):
        moved = [to_y(parts(k), k) for k in (2, 1, 3)]
        total = parts(0)
        for value in moved:
            total = total + value
        total = total.reshape(4, SHARE, B)
        arrived = None
        for k in range(4):
            value = send(pick(total, zh ^ k, 0), lambda x, c, y, h, l: (h ^ k, c, y, x, l))
            arrived = value if arrived is None else arrived + value
        return arrived

    def gather_rows(share):
        whole = ordered([share] + [to_x(share, k) for k in (1, 2, 3)], x)
        other = to_core(whole)
        return jnp.stack([jnp.where(core == 0, whole, other), jnp.where(core == 0, other, whole)])

    def sum_rows(partial_sum):
        view = partial_sum.reshape(HALF, 2, B)
        total = pick(view, core, 1) + to_core(pick(view, 1 - core, 1))
        total = total.reshape(4, SHARE, B)
        moved = [to_x(pick(total, x ^ k, 0), k) for k in (2, 1, 3)]
        arrived = pick(total, x, 0)
        for value in moved:
            arrived = arrived + value
        return arrived

    def share_to_rows(share):
        whole = ordered([send(share, lambda x, c, y, h, l: (h, c, y, x ^ k, l)) for k in range(4)], zh)
        moved = {k: to_y(whole, k) for k in (2, 1, 3)}
        return [whole, moved[1], moved[2], moved[3]]

    def block(number, k):
        return pick(blocks[number], y ^ k, 0)

    first = dot(right_side[0, 0], diag_inverse[0, 0], 1, 1, HIGHEST)
    halves = first.reshape(4, 2, SHARE, B)
    own_half = pick(halves, zl, 1).reshape(HALF, B)
    other_half = to_pair(pick(halves, 1 - zl, 1).reshape(HALF, B))
    columns = jnp.stack([jnp.where(zl == 0, own_half, other_half), jnp.where(zl == 0, other_half, own_half)])
    shares = [pick(pick(columns, core, 0).reshape(4, SHARE, B), x, 0)]
    forward = [jnp.concatenate([columns[0], columns[1]], 1)]
    forward_out = [first]
    for current in range(1, LV):

        def parts(k):
            total = None
            for earlier in range(current):
                term = dot(forward[earlier], block(pair_number(current, earlier), k), 1, 1)
                total = term if total is None else total + term
            return total

        share = dot(right_share[current] - update_to_share(parts), inverse[current], 1, 1, HIGHEST)
        shares.append(share)
        columns = gather_rows(share)
        forward.append(jnp.concatenate([columns[0], columns[1]], 1))
        kept = pick(columns, zl, 0).reshape(4, SHARE, B)
        other = to_pair(pick(columns, 1 - zl, 0)).reshape(4, SHARE, B)
        forward_out.append(by_pair(kept[:, None], other[:, None], 1).reshape(NRHS, B))

    solution = [None] * LV
    rows_of = [None] * LV
    for current in range(LV - 1, -1, -1):
        update = shares[current]
        if current < LV - 1:
            partial_sum = None
            for later_level in range(LV - 1, current, -1):
                for k in range(4):
                    term = dot(rows_of[later_level][k], block(pair_number(later_level, current), k), 1, 0)
                    partial_sum = term if partial_sum is None else partial_sum + term
            update = update - sum_rows(partial_sum)
        solved = dot(update, inverse[current], 1, 0, HIGHEST)
        solution[current] = swap(solved)
        if current > 0:
            rows_of[current] = share_to_rows(solved)

    return jnp.stack(forward_out)[:, None], jnp.stack(solution)[:, None]


def solution(mesh):
    in_specs = (
        P(None, None, "prow", "pcol", None, None),
        P(None, None, "prow", "pcol"),
        P(None, "pcol", None, None),
        P(None, "pcol", None, None),
    )
    out_specs = (P(None, "pcol", None, None), P(None, "pcol", "prow", None))
    return jax.shard_map(local, mesh=mesh, in_specs=in_specs, out_specs=out_specs, check_vma=False)
```

```python
import jax
import jax.numpy as jnp
from jax import lax
from jax.sharding import PartitionSpec as P

B = 256
NRHS = 512
LV = 4
SHARE = 64
HALF = 256
HIGH = lax.Precision.HIGH
HIGHEST = lax.Precision.HIGHEST

SHIFTED = (False, True, True, False)


def offset(shifted, low, half):
    return low * 0 if not shifted else half - low


def pair_number(later_level, earlier):
    return later_level * (later_level - 1) // 2 + earlier


def send(value, target):
    pairs = []
    for device in range(256):
        row, column = divmod(device, 32)
        there = target(row // 2, row % 2, column // 8, column // 2 % 4, column % 2)
        pairs.append((device, (there[0] * 2 + there[1]) * 32 + there[2] * 8 + there[3] * 2 + there[4]))
    return lax.ppermute(value, ("prow", "pcol"), pairs)


def to_y(value, k):
    return send(value, lambda x, c, y, h, l: (x, c, y ^ k, h, l))


def to_x(value, k):
    return send(value, lambda x, c, y, h, l: (x ^ k, c, y, h, l))


def to_core(value):
    return send(value, lambda x, c, y, h, l: (x, c ^ 1, y, h, l))


def to_pair(value, shifted):
    return send(value, lambda x, c, y, h, l: (x, c, y, (h - offset(shifted, l, l ^ 1)) % 4, l ^ 1))


def to_worker(value, shifted):
    return send(value, lambda x, c, y, h, l: (x, l, y, (h - offset(shifted, l, c)) % 4, c))


def from_worker(value, shifted):
    return send(value, lambda x, c, y, h, l: (x, l, y, (h + offset(shifted, c, l)) % 4, c))


def later(value, earlier):
    return value + 0.0 * earlier[(0,) * earlier.ndim]


def dot(left, right, left_axis, right_axis, precision=HIGH):
    return lax.dot_general(
        left,
        right,
        (((left_axis,), (right_axis,)), ((), ())),
        precision=precision,
        preferred_element_type=jnp.float32,
    )


def pick(value, index, axis):
    return lax.dynamic_index_in_dim(value, index, axis, keepdims=False)


def ordered(items, own):
    low, high = own % 2 == 1, own // 2 == 1
    pairs = [jnp.where(low, items[k ^ 1], items[k]) for k in range(4)]
    return jnp.concatenate([jnp.where(high, pairs[s ^ 2], pairs[s]) for s in range(4)])


def local(factor_blocks, block_pattern, right_side, diag_inverse):
    row = lax.axis_index("prow")
    column = lax.axis_index("pcol")
    x, core = row // 2, row % 2
    y, zh, zl = column // 8, column // 2 % 4, column % 2
    pattern = block_pattern[:, :, 0, 0].astype(jnp.float32)

    def by_pair(own, other, axis):
        return jnp.concatenate([jnp.where(zl == 0, own, other), jnp.where(zl == 0, other, own)], axis)

    def masked(number, earlier=()):
        weights = pattern[number]
        for item in earlier:
            weights = later(weights, item)
        return factor_blocks[number, :, 0, 0] * weights[:, None, None]

    own_blocks, other_blocks = {}, {}

    def exchange(number, earlier=()):
        shifted = SHIFTED[(0, 0, 1, 0, 1, 2)[number]]
        own_blocks[number] = masked(number, earlier)
        other_blocks[number] = to_pair(own_blocks[number], shifted)

    right = right_side[:, 0].reshape(LV, 8, SHARE, B)
    right_share, inverse = [None] * LV, [None] * LV

    def fetch(level, earlier=None):
        value = jnp.concatenate([diag_inverse[level, 0], pick(right[level], row, 0)])
        if earlier is not None:
            value = later(value, earlier)
        value = to_worker(value, SHIFTED[level])
        inverse[level], right_share[level] = value[:B], value[B:]

    exchange(0)
    fetch(1)
    exchange(2, (inverse[1],))
    exchange(1, (other_blocks[0],))
    fetch(2, other_blocks[2])
    fetch(3, other_blocks[1])
    fetch(0, other_blocks[1])
    blocks = {}

    def update_to_share(parts, shifted):
        moved = [to_y(parts(k), k) for k in (2, 1, 3)]
        total = parts(0)
        for value in moved:
            total = total + value
        total = total.reshape(4, SHARE, B)
        arrived = None
        for k in range(4):
            value = send(pick(total, zh ^ k, 0), lambda x, c, y, h, l: (h ^ k, c, y, (x - offset(shifted, c, l)) % 4, l))
            arrived = value if arrived is None else arrived + value
        return arrived

    def gather_rows(share):
        whole = ordered([share] + [to_x(share, k) for k in (1, 2, 3)], x)
        other = to_core(whole)
        return jnp.stack([jnp.where(core == 0, whole, other), jnp.where(core == 0, other, whole)])

    def sum_rows(partial_sum):
        view = partial_sum.reshape(HALF, 2, B)
        total = pick(view, core, 1) + to_core(pick(view, 1 - core, 1))
        total = total.reshape(4, SHARE, B)
        moved = [to_x(pick(total, x ^ k, 0), k) for k in (2, 1, 3)]
        arrived = pick(total, x, 0)
        for value in moved:
            arrived = arrived + value
        return arrived

    def share_to_rows(share, shifted):
        items = []
        for k in range(4):
            items.append(send(share, lambda x, c, y, h, l: ((h + offset(shifted, c, l)) % 4, c, y, x ^ k, l)))
        whole = ordered(items, zh)
        moved = {k: to_y(whole, k) for k in (2, 1, 3)}
        return [whole, moved[1], moved[2], moved[3]]

    def block(number, k):
        if number not in blocks:
            blocks[number] = by_pair(own_blocks[number], other_blocks[number], 2)
        return pick(blocks[number], y ^ k, 0)

    first = dot(right_side[0, 0], diag_inverse[0, 0], 1, 1, HIGHEST)
    halves = first.reshape(4, 2, SHARE, B)
    own_half = pick(halves, zl, 1).reshape(HALF, B)
    other_half = to_pair(pick(halves, 1 - zl, 1).reshape(HALF, B), SHIFTED[0])
    columns = jnp.stack([jnp.where(zl == 0, own_half, other_half), jnp.where(zl == 0, other_half, own_half)])
    shares = [pick(pick(columns, core, 0).reshape(4, SHARE, B), x, 0)]
    forward = [jnp.concatenate([columns[0], columns[1]], 1)]
    forward_out = [first]
    for current in range(1, LV):

        def parts(k):
            total = None
            for earlier in range(current):
                term = dot(forward[earlier], block(pair_number(current, earlier), k), 1, 1)
                total = term if total is None else total + term
            return total

        arrived = update_to_share(parts, SHIFTED[current])
        if current == 1:
            exchange(3, (other_blocks[1], arrived))
            exchange(4, (other_blocks[2], arrived))
            exchange(5, (other_blocks[4],))
        share = dot(right_share[current] - arrived, inverse[current], 1, 1, HIGHEST)
        shares.append(share)
        columns = gather_rows(share)
        forward.append(jnp.concatenate([columns[0], columns[1]], 1))
        kept = pick(columns, zl, 0).reshape(4, SHARE, B)
        other = to_pair(pick(columns, 1 - zl, 0), SHIFTED[current]).reshape(4, SHARE, B)
        forward_out.append(by_pair(kept[:, None], other[:, None], 1).reshape(NRHS, B))

    solution = [None] * LV
    rows_of = [None] * LV
    for current in range(LV - 1, -1, -1):
        update = shares[current]
        if current < LV - 1:
            partial_sum = None
            for later_level in range(LV - 1, current, -1):
                for k in range(4):
                    term = dot(rows_of[later_level][k], block(pair_number(later_level, current), k), 1, 0)
                    partial_sum = term if partial_sum is None else partial_sum + term
            update = update - sum_rows(partial_sum)
        solved = dot(update, inverse[current], 1, 0, HIGHEST)
        solution[current] = from_worker(solved, SHIFTED[current])
        if current > 0:
            rows_of[current] = share_to_rows(solved, SHIFTED[current])

    return jnp.stack(forward_out)[:, None], jnp.stack(solution)[:, None]


def solution(mesh):
    in_specs = (
        P(None, None, "prow", "pcol", None, None),
        P(None, None, "prow", "pcol"),
        P(None, "pcol", None, None),
        P(None, "pcol", None, None),
    )
    out_specs = (P(None, "pcol", None, None), P(None, "pcol", "prow", None))
    return jax.shard_map(local, mesh=mesh, in_specs=in_specs, out_specs=out_specs, check_vma=False)
```

```python
import jax
import jax.numpy as jnp
from jax import lax
from jax.sharding import PartitionSpec as P

B = 256
NRHS = 512
LV = 4
SHARE = 64
HALF = 256
HIGH = lax.Precision.HIGH
HIGHEST = lax.Precision.HIGHEST

SHIFTED = (False, True, True, False)


def offset(shifted, low, half):
    return low * 0 if not shifted else half - low


def pair_number(later_level, earlier):
    return later_level * (later_level - 1) // 2 + earlier


def send(value, target):
    pairs = []
    for device in range(256):
        row, column = divmod(device, 32)
        there = target(row // 2, row % 2, column // 8, column // 2 % 4, column % 2)
        pairs.append((device, (there[0] * 2 + there[1]) * 32 + there[2] * 8 + there[3] * 2 + there[4]))
    return lax.ppermute(value, ("prow", "pcol"), pairs)


def to_y(value, k):
    return send(value, lambda x, c, y, h, l: (x, c, y ^ k, h, l))


def to_x(value, k):
    return send(value, lambda x, c, y, h, l: (x ^ k, c, y, h, l))


def to_core(value):
    return send(value, lambda x, c, y, h, l: (x, c ^ 1, y, h, l))


def to_pair(value, shifted):
    return send(value, lambda x, c, y, h, l: (x, c, y, (h - offset(shifted, l, l ^ 1)) % 4, l ^ 1))


def to_worker(value, shifted):
    return send(value, lambda x, c, y, h, l: (x, l, y, (h - offset(shifted, l, c)) % 4, c))


def from_worker(value, shifted):
    return send(value, lambda x, c, y, h, l: (x, l, y, (h + offset(shifted, c, l)) % 4, c))


def later(value, earlier):
    return value + 0.0 * earlier[(0,) * earlier.ndim]


def dot(left, right, left_axis, right_axis, precision=HIGH):
    return lax.dot_general(
        left,
        right,
        (((left_axis,), (right_axis,)), ((), ())),
        precision=precision,
        preferred_element_type=jnp.float32,
    )


def pick(value, index, axis):
    return lax.dynamic_index_in_dim(value, index, axis, keepdims=False)


def ordered(items, own):
    low, high = own % 2 == 1, own // 2 == 1
    pairs = [jnp.where(low, items[k ^ 1], items[k]) for k in range(4)]
    return jnp.concatenate([jnp.where(high, pairs[s ^ 2], pairs[s]) for s in range(4)])


def local(factor_blocks, block_pattern, right_side, diag_inverse):
    row = lax.axis_index("prow")
    column = lax.axis_index("pcol")
    x, core = row // 2, row % 2
    y, zh, zl = column // 8, column // 2 % 4, column % 2
    pattern = block_pattern[:, :, 0, 0].astype(jnp.float32)

    own_low = core == zl

    def by_half(own, other, axis):
        return jnp.concatenate([jnp.where(zl == 0, own, other), jnp.where(zl == 0, other, own)], axis)

    def by_column(mine, others):
        return jnp.where(own_low, mine, others), jnp.where(own_low, others, mine)

    def masked(number, earlier=()):
        weights = pattern[number]
        for item in earlier:
            weights = later(weights, item)
        return factor_blocks[number, :, 0, 0] * weights[:, None, None]

    own_blocks, other_blocks = {}, {}

    def exchange(number, earlier=()):
        shifted = SHIFTED[(0, 0, 1, 0, 1, 2)[number]]
        own_blocks[number] = masked(number, earlier)
        other_blocks[number] = to_pair(own_blocks[number], shifted)

    right = right_side[:, 0].reshape(LV, 8, SHARE, B)
    right_share, inverse = [None] * LV, [None] * LV

    def fetch(level, earlier=None):
        value = jnp.concatenate([diag_inverse[level, 0], pick(right[level], row, 0)])
        if earlier is not None:
            value = later(value, earlier)
        value = to_worker(value, SHIFTED[level])
        inverse[level], right_share[level] = value[:B], value[B:]

    exchange(0)
    fetch(1)
    exchange(2, (other_blocks[0],))
    fetch(2, other_blocks[2])
    exchange(1, (other_blocks[2],))
    fetch(3, other_blocks[1])
    fetch(0, other_blocks[1])
    exchange(4, (other_blocks[1],))
    exchange(3, (other_blocks[4],))
    exchange(5, (other_blocks[4],))
    before_z_stage = {1: (2,), 2: (4,), 3: ()}
    before_core_stage = {1: (1,), 2: (3,), 3: ()}

    def update_to_share(parts, shifted, needed):
        moved = [to_y(parts(k), k) for k in (2, 1, 3)]
        total = parts(0)
        for value in moved:
            total = total + value
        for number in needed:
            total = later(total, other_blocks[number])
        total = total.reshape(4, SHARE, B)
        arrived = None
        for k in range(4):
            value = send(pick(total, zh ^ k, 0), lambda x, c, y, h, l: (h ^ k, c, y, (x - offset(shifted, c, l)) % 4, l))
            arrived = value if arrived is None else arrived + value
        return arrived

    def gather_rows(share, needed):
        whole = ordered([share] + [to_x(share, k) for k in (1, 2, 3)], x)
        for number in needed:
            whole = later(whole, other_blocks[number])
        return by_column(whole, to_core(whole))

    def sum_rows(own, other):
        mine, others = by_column(own, other)
        total = (mine + to_core(others)).reshape(4, SHARE, B)
        moved = [to_x(pick(total, x ^ k, 0), k) for k in (2, 1, 3)]
        arrived = pick(total, x, 0)
        for value in moved:
            arrived = arrived + value
        return arrived

    def share_to_rows(share, shifted):
        items = []
        for k in range(4):
            items.append(send(share, lambda x, c, y, h, l: ((h + offset(shifted, c, l)) % 4, c, y, x ^ k, l)))
        whole = ordered(items, zh)
        moved = {k: to_y(whole, k) for k in (2, 1, 3)}
        return [whole, moved[1], moved[2], moved[3]]

    def block(number, k):
        return pick(own_blocks[number], y ^ k, 0), pick(other_blocks[number], y ^ k, 0)

    first = dot(right_side[0, 0], diag_inverse[0, 0], 1, 1, HIGHEST)
    halves = first.reshape(4, 2, SHARE, B)
    own_half = pick(halves, zl, 1).reshape(HALF, B)
    other_half = to_pair(pick(halves, 1 - zl, 1).reshape(HALF, B), SHIFTED[0])
    shares = [pick(jnp.where(own_low, own_half, other_half).reshape(4, SHARE, B), x, 0)]
    forward = [(own_half, other_half)]
    forward_out = [first]
    for current in range(1, LV):

        def parts(k):
            total = None
            for earlier in range(current):
                for value, factor in zip(forward[earlier], block(pair_number(current, earlier), k)):
                    term = dot(value, factor, 1, 1)
                    total = term if total is None else total + term
            return total

        arrived = update_to_share(parts, SHIFTED[current], before_z_stage[current])
        share = dot(right_share[current] - arrived, inverse[current], 1, 1, HIGHEST)
        shares.append(share)
        own, other = gather_rows(share, before_core_stage[current])
        forward.append((own, other))
        other = to_pair(other, SHIFTED[current]).reshape(4, 1, SHARE, B)
        forward_out.append(by_half(own.reshape(4, 1, SHARE, B), other, 1).reshape(NRHS, B))

    solution = [None] * LV
    rows_of = [None] * LV
    for current in range(LV - 1, -1, -1):
        update = shares[current]
        if current < LV - 1:
            partial_sums = [None, None]
            for later_level in range(LV - 1, current, -1):
                for k in range(4):
                    for side, factor in enumerate(block(pair_number(later_level, current), k)):
                        term = dot(rows_of[later_level][k], factor, 1, 0)
                        partial_sums[side] = term if partial_sums[side] is None else partial_sums[side] + term
            update = update - sum_rows(*partial_sums)
        solved = dot(update, inverse[current], 1, 0, HIGHEST)
        solution[current] = from_worker(solved, SHIFTED[current])
        if current > 0:
            rows_of[current] = share_to_rows(solved, SHIFTED[current])

    return jnp.stack(forward_out)[:, None], jnp.stack(solution)[:, None]


def solution(mesh):
    in_specs = (
        P(None, None, "prow", "pcol", None, None),
        P(None, None, "prow", "pcol"),
        P(None, "pcol", None, None),
        P(None, "pcol", None, None),
    )
    out_specs = (P(None, "pcol", None, None), P(None, "pcol", "prow", None))
    return jax.shard_map(local, mesh=mesh, in_specs=in_specs, out_specs=out_specs, check_vma=False)
```

```python
import jax
import jax.numpy as jnp
from jax import lax
from jax.sharding import PartitionSpec as P

B = 256
NRHS = 512
LV = 4
SHARE = 64
HALF = 256
HIGH = lax.Precision.HIGH
HIGHEST = lax.Precision.HIGHEST

SHIFTED = (False, True, True, False)


def offset(shifted, low, half):
    return low * 0 if not shifted else half - low


def pair_number(later_level, earlier):
    return later_level * (later_level - 1) // 2 + earlier


def send(value, target):
    pairs = []
    for device in range(256):
        row, column = divmod(device, 32)
        there = target(row // 2, row % 2, column // 8, column // 2 % 4, column % 2)
        pairs.append((device, (there[0] * 2 + there[1]) * 32 + there[2] * 8 + there[3] * 2 + there[4]))
    return lax.ppermute(value, ("prow", "pcol"), pairs)


def to_y(value, k):
    return send(value, lambda x, c, y, h, l: (x, c, y ^ k, h, l))


def to_x(value, k):
    return send(value, lambda x, c, y, h, l: (x ^ k, c, y, h, l))


def to_core(value):
    return send(value, lambda x, c, y, h, l: (x, c ^ 1, y, h, l))


def to_pair(value, shifted):
    return send(value, lambda x, c, y, h, l: (x, c, y, (h - offset(shifted, l, l ^ 1)) % 4, l ^ 1))


def to_worker(value, shifted):
    return send(value, lambda x, c, y, h, l: (x, l, y, (h - offset(shifted, l, c)) % 4, c))


def from_worker(value, shifted):
    return send(value, lambda x, c, y, h, l: (x, l, y, (h + offset(shifted, c, l)) % 4, c))


def later(value, earlier):
    return value + 0.0 * earlier[(0,) * earlier.ndim]


def dot(left, right, left_axis, right_axis, precision=HIGH):
    return lax.dot_general(
        left,
        right,
        (((left_axis,), (right_axis,)), ((), ())),
        precision=precision,
        preferred_element_type=jnp.float32,
    )


def pick(value, index, axis):
    return lax.dynamic_index_in_dim(value, index, axis, keepdims=False)


def ordered(items, own):
    low, high = own % 2 == 1, own // 2 == 1
    pairs = [jnp.where(low, items[k ^ 1], items[k]) for k in range(4)]
    return jnp.concatenate([jnp.where(high, pairs[s ^ 2], pairs[s]) for s in range(4)])


def local(factor_blocks, block_pattern, right_side, diag_inverse):
    row = lax.axis_index("prow")
    column = lax.axis_index("pcol")
    x, core = row // 2, row % 2
    y, zh, zl = column // 8, column // 2 % 4, column % 2
    pattern = block_pattern[:, :, 0, 0].astype(jnp.float32)

    own_low = core == zl

    def by_half(own, other, axis):
        return jnp.concatenate([jnp.where(zl == 0, own, other), jnp.where(zl == 0, other, own)], axis)

    def by_column(mine, others):
        return jnp.where(own_low, mine, others), jnp.where(own_low, others, mine)

    def masked(number, earlier=()):
        weights = pattern[number]
        for item in earlier:
            weights = later(weights, item)
        return factor_blocks[number, :, 0, 0] * weights[:, None, None]

    own_blocks, other_blocks = {}, {}

    def exchange(number, earlier=()):
        shifted = SHIFTED[(0, 0, 1, 0, 1, 2)[number]]
        own_blocks[number] = masked(number, earlier)
        other_blocks[number] = to_pair(own_blocks[number], shifted)

    right = right_side[:, 0].reshape(LV, 8, SHARE, B)
    right_share, inverse = [None] * LV, [None] * LV

    def fetch(level, earlier=None):
        value = jnp.concatenate([diag_inverse[level, 0], pick(right[level], row, 0)])
        if earlier is not None:
            value = later(value, earlier)
        value = to_worker(value, SHIFTED[level])
        inverse[level], right_share[level] = value[:B], value[B:]

    exchange(0)
    fetch(1)
    exchange(2, (other_blocks[0],))
    exchange(1, (other_blocks[0],))
    fetch(2, other_blocks[2])
    fetch(3, other_blocks[1])
    fetch(0, other_blocks[1])
    exchange(4, (other_blocks[2],))
    exchange(5, (other_blocks[4],))
    before_z_stage = {1: (1, 2), 2: (3,), 3: ()}
    before_core_stage = {1: (4,), 2: (5,), 3: ()}

    def update_to_share(parts, shifted, needed):
        moved = [to_y(parts(k), k) for k in (2, 1, 3)]
        total = parts(0)
        for value in moved:
            total = total + value
        for number in needed:
            total = later(total, other_blocks[number])
        total = total.reshape(4, SHARE, B)
        arrived = None
        for k in range(4):
            value = send(pick(total, zh ^ k, 0), lambda x, c, y, h, l: (h ^ k, c, y, (x - offset(shifted, c, l)) % 4, l))
            arrived = value if arrived is None else arrived + value
        return arrived

    def gather_rows(share, needed):
        whole = ordered([share] + [to_x(share, k) for k in (1, 2, 3)], x)
        for number in needed:
            whole = later(whole, other_blocks[number])
        return by_column(whole, to_core(whole))

    def sum_rows(own, other):
        mine, others = by_column(own, other)
        total = (mine + to_core(others)).reshape(4, SHARE, B)
        moved = [to_x(pick(total, x ^ k, 0), k) for k in (2, 1, 3)]
        arrived = pick(total, x, 0)
        for value in moved:
            arrived = arrived + value
        return arrived

    def share_to_rows(share, shifted):
        items = []
        for k in range(4):
            items.append(send(share, lambda x, c, y, h, l: ((h + offset(shifted, c, l)) % 4, c, y, x ^ k, l)))
        whole = ordered(items, zh)
        moved = {k: to_y(whole, k) for k in (2, 1, 3)}
        return [whole, moved[1], moved[2], moved[3]]

    def block(number, k):
        return pick(own_blocks[number], y ^ k, 0), pick(other_blocks[number], y ^ k, 0)

    first = dot(right_side[0, 0], diag_inverse[0, 0], 1, 1, HIGHEST)
    halves = first.reshape(4, 2, SHARE, B)
    own_half = pick(halves, zl, 1).reshape(HALF, B)
    other_half = to_pair(pick(halves, 1 - zl, 1).reshape(HALF, B), SHIFTED[0])
    shares = [pick(jnp.where(own_low, own_half, other_half).reshape(4, SHARE, B), x, 0)]
    forward = [(own_half, other_half)]
    for current in range(1, LV):

        def parts(k):
            total = None
            for earlier in range(current):
                for value, factor in zip(forward[earlier], block(pair_number(current, earlier), k)):
                    term = dot(value, factor, 1, 1)
                    total = term if total is None else total + term
            return total

        arrived = update_to_share(parts, SHIFTED[current], before_z_stage[current])
        if current == 1:
            exchange(3, (other_blocks[1], arrived))
        share = dot(right_share[current] - arrived, inverse[current], 1, 1, HIGHEST)
        shares.append(share)
        own, other = gather_rows(share, before_core_stage[current])
        forward.append((own, other))

    def whole_forward(level, other):
        own = forward[level][0].reshape(4, 1, SHARE, B)
        return by_half(own, other.reshape(4, 1, SHARE, B), 1).reshape(NRHS, B)

    forward_out = [first] + [None] * (LV - 1)
    solution = [None] * LV
    rows_of = [None] * LV
    for current in range(LV - 1, -1, -1):
        update = shares[current]
        if current < LV - 1:
            partial_sums = [None, None]
            for later_level in range(LV - 1, current, -1):
                for k in range(4):
                    for side, factor in enumerate(block(pair_number(later_level, current), k)):
                        term = dot(rows_of[later_level][k], factor, 1, 0)
                        partial_sums[side] = term if partial_sums[side] is None else partial_sums[side] + term
            update = update - sum_rows(*partial_sums)
            update = later(later(update, solution[current + 1]), forward_other)
        solved = dot(update, inverse[current], 1, 0, HIGHEST)
        solution[current] = from_worker(solved, SHIFTED[current])
        if current > 0:
            forward_other = to_pair(later(forward[current][1], solved), SHIFTED[current])
            forward_out[current] = whole_forward(current, forward_other)
            rows_of[current] = share_to_rows(solved, SHIFTED[current])

    return jnp.stack(forward_out)[:, None], jnp.stack(solution)[:, None]


def solution(mesh):
    in_specs = (
        P(None, None, "prow", "pcol", None, None),
        P(None, None, "prow", "pcol"),
        P(None, "pcol", None, None),
        P(None, "pcol", None, None),
    )
    out_specs = (P(None, "pcol", None, None), P(None, "pcol", "prow", None))
    return jax.shard_map(local, mesh=mesh, in_specs=in_specs, out_specs=out_specs, check_vma=False)
```

```python
import jax
import jax.numpy as jnp
from jax import lax
from jax.sharding import PartitionSpec as P

B = 256
NRHS = 512
LV = 4
SHARE = 64
HALF = 256
HIGH = lax.Precision.HIGH
HIGHEST = lax.Precision.HIGHEST

SHIFTED = (False, True, True, False)


def offset(shifted, low, half):
    return low * 0 if not shifted else half - low


def pair_number(later_level, earlier):
    return later_level * (later_level - 1) // 2 + earlier


def send(value, target):
    pairs = []
    for device in range(256):
        row, column = divmod(device, 32)
        there = target(row // 2, row % 2, column // 8, column // 2 % 4, column % 2)
        pairs.append((device, (there[0] * 2 + there[1]) * 32 + there[2] * 8 + there[3] * 2 + there[4]))
    return lax.ppermute(value, ("prow", "pcol"), pairs)


def to_y(value, k):
    return send(value, lambda x, c, y, h, l: (x, c, y ^ k, h, l))


def to_x(value, k):
    return send(value, lambda x, c, y, h, l: (x ^ k, c, y, h, l))


def to_core(value):
    return send(value, lambda x, c, y, h, l: (x, c ^ 1, y, h, l))


def to_pair(value, shifted):
    return send(value, lambda x, c, y, h, l: (x, c, y, (h - offset(shifted, l, l ^ 1)) % 4, l ^ 1))


def to_worker(value, shifted):
    return send(value, lambda x, c, y, h, l: (x, l, y, (h - offset(shifted, l, c)) % 4, c))


def from_worker(value, shifted):
    return send(value, lambda x, c, y, h, l: (x, l, y, (h + offset(shifted, c, l)) % 4, c))


def later(value, earlier):
    return value + 0.0 * earlier[(0,) * earlier.ndim]


def dot(left, right, left_axis, right_axis, precision=HIGH):
    return lax.dot_general(
        left,
        right,
        (((left_axis,), (right_axis,)), ((), ())),
        precision=precision,
        preferred_element_type=jnp.float32,
    )


def pick(value, index, axis):
    return lax.dynamic_index_in_dim(value, index, axis, keepdims=False)


def ordered(items, own):
    low, high = own % 2 == 1, own // 2 == 1
    pairs = [jnp.where(low, items[k ^ 1], items[k]) for k in range(4)]
    return jnp.concatenate([jnp.where(high, pairs[s ^ 2], pairs[s]) for s in range(4)])


def local(factor_blocks, block_pattern, right_side, diag_inverse):
    row = lax.axis_index("prow")
    column = lax.axis_index("pcol")
    x, core = row // 2, row % 2
    y, zh, zl = column // 8, column // 2 % 4, column % 2
    pattern = block_pattern[:, :, 0, 0].astype(jnp.float32)

    own_low = core == zl

    def by_half(own, other, axis):
        return jnp.concatenate([jnp.where(zl == 0, own, other), jnp.where(zl == 0, other, own)], axis)

    def by_column(mine, others):
        return jnp.where(own_low, mine, others), jnp.where(own_low, others, mine)

    def masked(number, earlier=()):
        weights = pattern[number]
        for item in earlier:
            weights = later(weights, item)
        return factor_blocks[number, :, 0, 0] * weights[:, None, None]

    own_blocks, other_blocks = {}, {}

    def exchange(number, earlier=()):
        shifted = SHIFTED[(0, 0, 1, 0, 1, 2)[number]]
        own_blocks[number] = masked(number, earlier)
        other_blocks[number] = to_pair(own_blocks[number], shifted)

    right = right_side[:, 0].reshape(LV, 8, SHARE, B)
    right_share, inverse = [None] * LV, [None] * LV

    def fetch(level, earlier=None):
        value = jnp.concatenate([diag_inverse[level, 0], pick(right[level], row, 0)])
        if earlier is not None:
            value = later(value, earlier)
        value = to_worker(value, SHIFTED[level])
        inverse[level], right_share[level] = value[:B], value[B:]

    exchange(0)
    exchange(2)
    fetch(1)
    exchange(1, (other_blocks[0],))
    exchange(4, (other_blocks[2],))
    fetch(2, other_blocks[1])
    fetch(3, other_blocks[1])
    fetch(0, other_blocks[1])
    before_z_stage = {1: (1, 4), 2: (3, 5), 3: ()}

    def update_to_share(parts, shifted, needed):
        moved = [to_y(parts(k), k) for k in (2, 1, 3)]
        total = parts(0)
        for value in moved:
            total = total + value
        for number in needed:
            total = later(total, other_blocks[number])
        total = total.reshape(4, SHARE, B)
        arrived = None
        for k in range(4):
            value = send(pick(total, zh ^ k, 0), lambda x, c, y, h, l: (h ^ k, c, y, (x - offset(shifted, c, l)) % 4, l))
            arrived = value if arrived is None else arrived + value
        return arrived

    def gather_rows(share):
        whole = ordered([share] + [to_x(share, k) for k in (1, 2, 3)], x)
        return by_column(whole, to_core(whole))

    def sum_rows(own, other):
        mine, others = by_column(own, other)
        total = (mine + to_core(others)).reshape(4, SHARE, B)
        moved = [to_x(pick(total, x ^ k, 0), k) for k in (2, 1, 3)]
        arrived = pick(total, x, 0)
        for value in moved:
            arrived = arrived + value
        return arrived

    def share_to_rows(share, shifted):
        items = []
        for k in range(4):
            items.append(send(share, lambda x, c, y, h, l: ((h + offset(shifted, c, l)) % 4, c, y, x ^ k, l)))
        whole = ordered(items, zh)
        moved = {k: to_y(whole, k) for k in (2, 1, 3)}
        return [whole, moved[1], moved[2], moved[3]]

    def block(number, k):
        return pick(own_blocks[number], y ^ k, 0), pick(other_blocks[number], y ^ k, 0)

    first = dot(right_side[0, 0], diag_inverse[0, 0], 1, 1, HIGHEST)
    halves = first.reshape(4, 2, SHARE, B)
    own_half = pick(halves, zl, 1).reshape(HALF, B)
    other_half = to_pair(pick(halves, 1 - zl, 1).reshape(HALF, B), SHIFTED[0])
    shares = [pick(jnp.where(own_low, own_half, other_half).reshape(4, SHARE, B), x, 0)]
    forward = [(own_half, other_half)]
    for current in range(1, LV):

        def parts(k):
            total = None
            for earlier in range(current):
                for value, factor in zip(forward[earlier], block(pair_number(current, earlier), k)):
                    term = dot(value, factor, 1, 1)
                    total = term if total is None else total + term
            return total

        arrived = update_to_share(parts, SHIFTED[current], before_z_stage[current])
        if current == 1:
            exchange(3, (arrived,))
            exchange(5, (arrived,))
        share = dot(right_share[current] - arrived, inverse[current], 1, 1, HIGHEST)
        shares.append(share)
        own, other = gather_rows(share)
        forward.append((own, other))

    def whole_forward(level, other):
        own = forward[level][0].reshape(4, 1, SHARE, B)
        return by_half(own, other.reshape(4, 1, SHARE, B), 1).reshape(NRHS, B)

    forward_out = [first] + [None] * (LV - 1)
    solution = [None] * LV
    rows_of = [None] * LV
    for current in range(LV - 1, -1, -1):
        update = shares[current]
        if current < LV - 1:
            partial_sums = [None, None]
            for later_level in range(LV - 1, current, -1):
                for k in range(4):
                    for side, factor in enumerate(block(pair_number(later_level, current), k)):
                        term = dot(rows_of[later_level][k], factor, 1, 0)
                        partial_sums[side] = term if partial_sums[side] is None else partial_sums[side] + term
            update = update - sum_rows(*partial_sums)
            update = later(later(update, solution[current + 1]), forward_other)
        solved = dot(update, inverse[current], 1, 0, HIGHEST)
        solution[current] = from_worker(solved, SHIFTED[current])
        if current > 0:
            forward_other = to_pair(later(forward[current][1], solved), SHIFTED[current])
            forward_out[current] = whole_forward(current, forward_other)
            rows_of[current] = share_to_rows(solved, SHIFTED[current])

    return jnp.stack(forward_out)[:, None], jnp.stack(solution)[:, None]


def solution(mesh):
    in_specs = (
        P(None, None, "prow", "pcol", None, None),
        P(None, None, "prow", "pcol"),
        P(None, "pcol", None, None),
        P(None, "pcol", None, None),
    )
    out_specs = (P(None, "pcol", None, None), P(None, "pcol", "prow", None))
    return jax.shard_map(local, mesh=mesh, in_specs=in_specs, out_specs=out_specs, check_vma=False)
```

```python
import jax
import jax.numpy as jnp
from jax import lax
from jax.sharding import PartitionSpec as P

B = 256
NRHS = 512
LV = 4
SHARE = 64
HALF = 256
HIGH = lax.Precision.HIGH
HIGHEST = lax.Precision.HIGHEST

SHIFTED = (False, True, True, False)


def offset(shifted, low, half):
    return low * 0 if not shifted else half - low


def pair_number(later_level, earlier):
    return later_level * (later_level - 1) // 2 + earlier


def send(value, target):
    pairs = []
    for device in range(256):
        row, column = divmod(device, 32)
        there = target(row // 2, row % 2, column // 8, column // 2 % 4, column % 2)
        pairs.append((device, (there[0] * 2 + there[1]) * 32 + there[2] * 8 + there[3] * 2 + there[4]))
    return lax.ppermute(value, ("prow", "pcol"), pairs)


def to_y(value, k):
    return send(value, lambda x, c, y, h, l: (x, c, y ^ k, h, l))


def to_x(value, k):
    return send(value, lambda x, c, y, h, l: (x ^ k, c, y, h, l))


def to_core(value):
    return send(value, lambda x, c, y, h, l: (x, c ^ 1, y, h, l))


def to_pair(value, shifted):
    return send(value, lambda x, c, y, h, l: (x, c, y, (h - offset(shifted, l, l ^ 1)) % 4, l ^ 1))


def to_worker(value, shifted):
    return send(value, lambda x, c, y, h, l: (x, l, y, (h - offset(shifted, l, c)) % 4, c))


def from_worker(value, shifted):
    return send(value, lambda x, c, y, h, l: (x, l, y, (h + offset(shifted, c, l)) % 4, c))


def later(value, earlier):
    return value + 0.0 * earlier[(0,) * earlier.ndim]


def dot(left, right, left_axis, right_axis, precision=HIGH):
    return lax.dot_general(
        left,
        right,
        (((left_axis,), (right_axis,)), ((), ())),
        precision=precision,
        preferred_element_type=jnp.float32,
    )


def pick(value, index, axis):
    return lax.dynamic_index_in_dim(value, index, axis, keepdims=False)


def ordered(items, own):
    low, high = own % 2 == 1, own // 2 == 1
    pairs = [jnp.where(low, items[k ^ 1], items[k]) for k in range(4)]
    return jnp.concatenate([jnp.where(high, pairs[s ^ 2], pairs[s]) for s in range(4)])


def local(factor_blocks, block_pattern, right_side, diag_inverse):
    row = lax.axis_index("prow")
    column = lax.axis_index("pcol")
    x, core = row // 2, row % 2
    y, zh, zl = column // 8, column // 2 % 4, column % 2
    pattern = block_pattern[:, :, 0, 0].astype(jnp.float32)

    own_low = core == zl

    def by_half(own, other, axis):
        return jnp.concatenate([jnp.where(zl == 0, own, other), jnp.where(zl == 0, other, own)], axis)

    def by_column(mine, others):
        return jnp.where(own_low, mine, others), jnp.where(own_low, others, mine)

    def masked(number, earlier=()):
        weights = pattern[number]
        for item in earlier:
            weights = later(weights, item)
        return factor_blocks[number, :, 0, 0] * weights[:, None, None]

    own_blocks, other_blocks = {}, {}

    def exchange(number, earlier=()):
        shifted = SHIFTED[(0, 0, 1, 0, 1, 2)[number]]
        own_blocks[number] = masked(number, earlier)
        other_blocks[number] = to_pair(own_blocks[number], shifted)

    right = right_side[:, 0].reshape(LV, 8, SHARE, B)
    right_share, inverse = [None] * LV, [None] * LV

    def fetch(level, earlier=None):
        value = jnp.concatenate([diag_inverse[level, 0], pick(right[level], row, 0)])
        if earlier is not None:
            value = later(value, earlier)
        value = to_worker(value, SHIFTED[level])
        inverse[level], right_share[level] = value[:B], value[B:]

    exchange(0)
    exchange(2)
    fetch(1)
    exchange(1, (other_blocks[0],))
    exchange(4, (other_blocks[2],))
    fetch(2, other_blocks[1])
    fetch(3, other_blocks[1])
    fetch(0, other_blocks[1])
    before_z_stage = {1: (1, 4), 2: (3, 5), 3: ()}

    def update_to_share(parts, shifted, needed):
        moved = [to_y(parts(k), k) for k in (1, 3, 2)]
        total = parts(0)
        for value in moved:
            total = total + value
        for number in needed:
            total = later(total, other_blocks[number])
        total = total.reshape(4, SHARE, B)
        arrived = None
        for k in range(4):
            value = send(pick(total, zh ^ k, 0), lambda x, c, y, h, l: (h ^ k, c, y, (x - offset(shifted, c, l)) % 4, l))
            arrived = value if arrived is None else arrived + value
        return arrived

    def gather_rows(share):
        whole = ordered([share] + [to_x(share, k) for k in (1, 2, 3)], x)
        return by_column(whole, to_core(whole))

    def sum_rows(own, other):
        mine, others = by_column(own, other)
        total = (mine + to_core(others)).reshape(4, SHARE, B)
        moved = [to_x(pick(total, x ^ k, 0), k) for k in (1, 3, 2)]
        arrived = pick(total, x, 0)
        for value in moved:
            arrived = arrived + value
        return arrived

    def share_to_rows(share, shifted):
        items = []
        for k in range(4):
            items.append(send(share, lambda x, c, y, h, l: ((h + offset(shifted, c, l)) % 4, c, y, x ^ k, l)))
        whole = ordered(items, zh)
        moved = {k: to_y(whole, k) for k in (1, 3, 2)}
        return [whole, moved[1], moved[2], moved[3]]

    def block(number, k):
        return pick(own_blocks[number], y ^ k, 0), pick(other_blocks[number], y ^ k, 0)

    first = dot(right_side[0, 0], diag_inverse[0, 0], 1, 1, HIGHEST)
    halves = first.reshape(4, 2, SHARE, B)
    own_half = pick(halves, zl, 1).reshape(HALF, B)
    other_half = to_pair(pick(halves, 1 - zl, 1).reshape(HALF, B), SHIFTED[0])
    shares = [pick(jnp.where(own_low, own_half, other_half).reshape(4, SHARE, B), x, 0)]
    forward = [(own_half, other_half)]
    for current in range(1, LV):

        def parts(k):
            total = None
            for earlier in range(current):
                for value, factor in zip(forward[earlier], block(pair_number(current, earlier), k)):
                    term = dot(value, factor, 1, 1)
                    total = term if total is None else total + term
            return total

        arrived = update_to_share(parts, SHIFTED[current], before_z_stage[current])
        if current == 1:
            exchange(3, (arrived,))
            exchange(5, (arrived,))
        share = dot(right_share[current] - arrived, inverse[current], 1, 1, HIGHEST)
        shares.append(share)
        own, other = gather_rows(share)
        forward.append((own, other))

    def whole_forward(level, other):
        own = forward[level][0].reshape(4, 1, SHARE, B)
        return by_half(own, other.reshape(4, 1, SHARE, B), 1).reshape(NRHS, B)

    forward_out = [first] + [None] * (LV - 1)
    solution = [None] * LV
    rows_of = [None] * LV
    for current in range(LV - 1, -1, -1):
        update = shares[current]
        if current < LV - 1:
            partial_sums = [None, None]
            for later_level in range(LV - 1, current, -1):
                for k in (0, 1, 3, 2):
                    for side, factor in enumerate(block(pair_number(later_level, current), k)):
                        term = dot(rows_of[later_level][k], factor, 1, 0)
                        partial_sums[side] = term if partial_sums[side] is None else partial_sums[side] + term
            update = update - sum_rows(*partial_sums)
            update = later(later(update, solution[current + 1]), forward_other)
        solved = dot(update, inverse[current], 1, 0, HIGHEST)
        solution[current] = from_worker(solved, SHIFTED[current])
        if current > 0:
            forward_other = to_pair(later(forward[current][1], solved), SHIFTED[current])
            forward_out[current] = whole_forward(current, forward_other)
            rows_of[current] = share_to_rows(solved, SHIFTED[current])

    return jnp.stack(forward_out)[:, None], jnp.stack(solution)[:, None]


def solution(mesh):
    in_specs = (
        P(None, None, "prow", "pcol", None, None),
        P(None, None, "prow", "pcol"),
        P(None, "pcol", None, None),
        P(None, "pcol", None, None),
    )
    out_specs = (P(None, "pcol", None, None), P(None, "pcol", "prow", None))
    return jax.shard_map(local, mesh=mesh, in_specs=in_specs, out_specs=out_specs, check_vma=False)
```

```python
import jax
import jax.numpy as jnp
from jax import lax
from jax.sharding import PartitionSpec as P

B = 256
NRHS = 512
LV = 4
SHARE = 64
HALF = 256
HIGH = lax.Precision.HIGH
HIGHEST = lax.Precision.HIGHEST

SHIFTED = (False, True, True, False)


def offset(shifted, low, half):
    return low * 0 if not shifted else half - low


def pair_number(later_level, earlier):
    return later_level * (later_level - 1) // 2 + earlier


def send(value, target):
    pairs = []
    for device in range(256):
        row, column = divmod(device, 32)
        there = target(row // 2, row % 2, column // 8, column // 2 % 4, column % 2)
        pairs.append((device, (there[0] * 2 + there[1]) * 32 + there[2] * 8 + there[3] * 2 + there[4]))
    return lax.ppermute(value, ("prow", "pcol"), pairs)


def to_y(value, k):
    return send(value, lambda x, c, y, h, l: (x, c, y ^ k, h, l))


def to_x(value, k):
    return send(value, lambda x, c, y, h, l: (x ^ k, c, y, h, l))


def to_core(value):
    return send(value, lambda x, c, y, h, l: (x, c ^ 1, y, h, l))


def to_pair(value, shifted):
    return send(value, lambda x, c, y, h, l: (x, c, y, (h - offset(shifted, l, l ^ 1)) % 4, l ^ 1))


def to_worker(value, shifted):
    return send(value, lambda x, c, y, h, l: (x, l, y, (h - offset(shifted, l, c)) % 4, c))


def from_worker(value, shifted):
    return send(value, lambda x, c, y, h, l: (x, l, y, (h + offset(shifted, c, l)) % 4, c))


def later(value, earlier):
    return value + 0.0 * earlier[(0,) * earlier.ndim]


def dot(left, right, left_axis, right_axis, precision=HIGH):
    return lax.dot_general(
        left,
        right,
        (((left_axis,), (right_axis,)), ((), ())),
        precision=precision,
        preferred_element_type=jnp.float32,
    )


def pick(value, index, axis):
    return lax.dynamic_index_in_dim(value, index, axis, keepdims=False)


def ordered(items, own):
    low, high = own % 2 == 1, own // 2 == 1
    pairs = [jnp.where(low, items[k ^ 1], items[k]) for k in range(4)]
    return jnp.concatenate([jnp.where(high, pairs[s ^ 2], pairs[s]) for s in range(4)])


def local(factor_blocks, block_pattern, right_side, diag_inverse):
    row = lax.axis_index("prow")
    column = lax.axis_index("pcol")
    x, core = row // 2, row % 2
    y, zh, zl = column // 8, column // 2 % 4, column % 2
    pattern = block_pattern[:, :, 0, 0].astype(jnp.float32)

    own_low = core == zl

    def by_half(own, other, axis):
        return jnp.concatenate([jnp.where(zl == 0, own, other), jnp.where(zl == 0, other, own)], axis)

    def by_column(mine, others):
        return jnp.where(own_low, mine, others), jnp.where(own_low, others, mine)

    def masked(number, earlier=()):
        weights = pattern[number]
        for item in earlier:
            weights = later(weights, item)
        return factor_blocks[number, :, 0, 0] * weights[:, None, None]

    own_blocks, other_blocks = {}, {}

    def exchange(number, earlier=()):
        shifted = SHIFTED[(0, 0, 1, 0, 1, 2)[number]]
        own_blocks[number] = masked(number, earlier)
        other_blocks[number] = to_pair(own_blocks[number], shifted)

    right = right_side[:, 0].reshape(LV, 8, SHARE, B)
    right_share, inverse = [None] * LV, [None] * LV

    def fetch(level, earlier=None):
        value = jnp.concatenate([diag_inverse[level, 0], pick(right[level], row, 0)])
        if earlier is not None:
            value = later(value, earlier)
        value = to_worker(value, SHIFTED[level])
        inverse[level], right_share[level] = value[:B], value[B:]

    exchange(0)
    exchange(2)
    fetch(1)
    exchange(1, (other_blocks[0],))
    exchange(4, (other_blocks[2],))
    fetch(2, other_blocks[1])
    fetch(3, other_blocks[1])
    fetch(0, other_blocks[1])
    before_z_stage = {1: (1, 4), 2: (3, 5), 3: ()}

    def update_to_share(parts, shifted, needed):
        moved = [to_y(parts(k), k) for k in (1, 3, 2)]
        total = parts(0)
        for value in moved:
            total = total + value
        for number in needed:
            total = later(total, other_blocks[number])
        total = total.reshape(4, SHARE, B)
        arrived = None
        for k in range(4):
            value = send(pick(total, zh ^ k, 0), lambda x, c, y, h, l: (h ^ k, c, y, (x - offset(shifted, c, l)) % 4, l))
            arrived = value if arrived is None else arrived + value
        return arrived

    def gather_rows(share):
        whole = ordered([share] + [to_x(share, k) for k in (1, 2, 3)], x)
        return by_column(whole, to_core(whole))

    def sum_rows(own, other):
        mine, others = by_column(own, other)
        total = (mine + to_core(others)).reshape(4, SHARE, B)
        moved = [to_x(pick(total, x ^ k, 0), k) for k in (1, 3, 2)]
        arrived = pick(total, x, 0)
        for value in moved:
            arrived = arrived + value
        return arrived

    def share_to_rows(share, shifted):
        items = []
        for k in range(4):
            items.append(send(share, lambda x, c, y, h, l: ((h + offset(shifted, c, l)) % 4, c, y, x ^ k, l)))
        whole = ordered(items, zh)
        moved = {k: to_y(whole, k) for k in (1, 3, 2)}
        return [whole, moved[1], moved[2], moved[3]]

    def block(number, k):
        return pick(own_blocks[number], y ^ k, 0), pick(other_blocks[number], y ^ k, 0)

    first = dot(right_side[0, 0], diag_inverse[0, 0], 1, 1, HIGHEST)
    halves = first.reshape(4, 2, SHARE, B)
    own_half = pick(halves, zl, 1).reshape(HALF, B)
    other_half = to_pair(pick(halves, 1 - zl, 1).reshape(HALF, B), SHIFTED[0])
    shares = [pick(jnp.where(own_low, own_half, other_half).reshape(4, SHARE, B), x, 0)]
    forward = [(own_half, other_half)]
    for current in range(1, LV):

        def parts(k):
            total = None
            for earlier in range(current):
                for value, factor in zip(forward[earlier], block(pair_number(current, earlier), k)):
                    term = dot(value, factor, 1, 1)
                    total = term if total is None else total + term
            return total

        arrived = update_to_share(parts, SHIFTED[current], before_z_stage[current])
        if current == 1:
            exchange(3, (arrived,))
            exchange(5, (arrived,))
        share = dot(right_share[current] - arrived, inverse[current], 1, 1, HIGHEST)
        shares.append(share)
        own, other = gather_rows(share)
        forward.append((own, other))

    def whole_forward(level, other):
        own = forward[level][0].reshape(4, 1, SHARE, B)
        return by_half(own, other.reshape(4, 1, SHARE, B), 1).reshape(NRHS, B)

    forward_out = [first] + [None] * (LV - 1)
    solution = [None] * LV
    rows_of = [None] * LV
    for current in range(LV - 1, -1, -1):
        update = shares[current]
        if current < LV - 1:
            partial_sums = [None, None]
            for later_level in range(LV - 1, current, -1):
                for k in (0, 1, 3, 2):
                    for side, factor in enumerate(block(pair_number(later_level, current), k)):
                        term = dot(rows_of[later_level][k], factor, 1, 0)
                        partial_sums[side] = term if partial_sums[side] is None else partial_sums[side] + term
            update = update - sum_rows(*partial_sums)
        solved = dot(update, inverse[current], 1, 0, HIGHEST)
        if current == 0:
            solution[current] = from_worker(solved, SHIFTED[current])
        else:
            if current < LV - 1:
                solved = later(later(solved, solution[current + 1]), forward_other)
            rows_of[current] = share_to_rows(solved, SHIFTED[current])
            there = rows_of[current][2]
            solution[current] = from_worker(later(solved, there), SHIFTED[current])
            forward_other = to_pair(later(forward[current][1], there), SHIFTED[current])
            forward_out[current] = whole_forward(current, forward_other)

    return jnp.stack(forward_out)[:, None], jnp.stack(solution)[:, None]


def solution(mesh):
    in_specs = (
        P(None, None, "prow", "pcol", None, None),
        P(None, None, "prow", "pcol"),
        P(None, "pcol", None, None),
        P(None, "pcol", None, None),
    )
    out_specs = (P(None, "pcol", None, None), P(None, "pcol", "prow", None))
    return jax.shard_map(local, mesh=mesh, in_specs=in_specs, out_specs=out_specs, check_vma=False)
```
